32 devices in a mesh: seq: 16 (over z, x, core), head: 2 (over y).
Axes of the slice: x: 2, y: 2, z: 4, core: 2. Of those that a mesh axis runs over, the one named last changes fastest.
Arguments:
- query_tokens: bfloat16 [2, 8192, 1024], P(None, 'seq', 'head'), may hold values from -6 to 6
- key_tokens: bfloat16 [2, 8192, 1024], P(None, 'seq', 'head'), may hold values from -16 to 16
- value_tokens: bfloat16 [2, 8192, 1024], P(None, 'seq', 'head'), may hold values from -16 to 16
- token_rates: float32 [3, 2, 4, 8192], P(None, None, 'head', 'seq'), may hold values from 0.1 to 1
- fast_init: bfloat16 [3, 4, 256, 256], P(None, 'head'), may hold values from -0.375 to 0.375
Outputs:
- mixer_out: bfloat16 [2, 8192, 1024], P(None, ('seq', 'head'))
The draws below stay inside these ranges and needn't reach their ends.
All inputs are finite; a program needn't handle non-finite values.
Results may differ from the reference program's by a relative error of at most 0.017.
Values may be sent and summed in bfloat16 or wider, within the bound.
A program may use at most 64 MiB of HBM per device.

```python
import math
import jax
import jax.numpy as jnp
from jax import lax

HD = 256
GROUPS = 2
HEADS = 4
GROUP = 8192


def feature_draw(key, salt):
    full_shape = (GROUPS, GROUP, HEADS * HD)
    key_scale, key_base = jax.random.split(jax.random.fold_in(key, salt), 2)
    scales = jnp.exp(jax.random.uniform(key_scale, (full_shape[-1],), jnp.float32, jnp.log(0.4), jnp.log(4.0)))
    result = jnp.clip(jax.random.normal(key_base, full_shape, jnp.float32), -4.0, 4.0) * scales
    return result.astype(jnp.bfloat16)


def draw_key_tokens(key, part):
    return feature_draw(key, 11)


def draw_value_tokens(key, part):
    return feature_draw(key, 23)


def levels(stream_key, extent, cuts, low, high):
    level, own = 1.0, jax.random.fold_in(stream_key, 6)
    for dim, shards_of in cuts:
        heights = jnp.exp(jax.random.uniform(jax.random.fold_in(own, dim), (shards_of,), jnp.float32, low / len(cuts), high / len(cuts)))
        level = level * jnp.repeat(heights, extent[dim] // shards_of).reshape([-1 if axis == dim else 1 for axis in range(len(extent))])
    return level


def bell_draw(rng, extent, spread, limit, cuts=(), kind=jnp.bfloat16):
    gain = levels(rng, extent, cuts, -0.22, 0.18) if cuts else 1.0
    values = jax.random.normal(rng, extent, jnp.float32) * spread * gain
    return jnp.minimum(jnp.maximum(values, -limit), limit).astype(kind)


def setup_inputs(seed: int = 0) -> dict:
    keys = jax.random.split(jax.random.key(seed), 6)
    query_tokens = bell_draw(keys[0], (GROUPS, GROUP, HEADS * HD), 1.0, 6.0, ((1, 16), (2, 2)))
    key_tokens = draw_key_tokens(jax.random.fold_in(keys[5], 71), 0)
    value_tokens = draw_value_tokens(jax.random.fold_in(keys[5], 71), 0)
    token_rates = jnp.clip(jnp.exp(math.log(1.0) - 2.3025851 * jax.random.uniform(keys[3], (3, GROUPS, HEADS, GROUP), jnp.float32) ** levels(keys[3], (3, GROUPS, HEADS, GROUP), ((2, 2), (3, 16)), -0.2, 0.2)), 0.1, 1.0)
    fast_init = bell_draw(keys[4], (3, HEADS, HD, HD), HD ** -0.5, 0.375, ((1, 2),))
    return dict(query_tokens=query_tokens, key_tokens=key_tokens, value_tokens=value_tokens, token_rates=token_rates, fast_init=fast_init)


step_size = 0.05
eps_grad = 1e-05
eps_row = 1e-06

def one_head(inputs):
    query_rows, key_rows, value_rows, rate_rows, weight_init = inputs
    fast_state = weight_init.astype(jnp.float32)
    target = jnp.sqrt(lax.optimization_barrier(jnp.mean(fast_state * fast_state, axis=-1, keepdims=True)))
    results = []
    for block_index in range(GROUPS):
        keys_now = key_rows[block_index]
        values_now = value_rows[block_index]
        current = fast_state.astype(jnp.bfloat16)
        gate_proj = jnp.dot(keys_now, current[0], preferred_element_type=jnp.float32)
        up_proj = jnp.dot(keys_now, current[1], preferred_element_type=jnp.float32)
        sigmoid_gate = jax.nn.sigmoid(gate_proj)
        silu_gate = gate_proj * sigmoid_gate
        hidden = (silu_gate * up_proj).astype(jnp.bfloat16)
        scaled_hidden = (hidden.astype(jnp.float32) * rate_rows[2, block_index][:, None]).astype(jnp.bfloat16)
        grad_down = -jnp.dot(scaled_hidden.T, values_now, preferred_element_type=jnp.float32)
        hidden_grad = -jnp.dot(values_now, current[2].T, preferred_element_type=jnp.float32)
        gate_grad = hidden_grad * up_proj * sigmoid_gate * (1.0 + gate_proj * (1.0 - sigmoid_gate))
        up_grad = hidden_grad * silu_gate
        gate_scaled = (gate_grad * rate_rows[0, block_index][:, None]).astype(jnp.bfloat16)
        up_scaled = (up_grad * rate_rows[1, block_index][:, None]).astype(jnp.bfloat16)
        grad_gate = jnp.dot(keys_now.T, gate_scaled, preferred_element_type=jnp.float32)
        grad_up = jnp.dot(keys_now.T, up_scaled, preferred_element_type=jnp.float32)
        gradients_now = jnp.stack([grad_gate, grad_up, grad_down])
        grad_rms = jnp.sqrt(lax.optimization_barrier(jnp.mean(gradients_now * gradients_now, axis=(1, 2), keepdims=True)) + eps_grad)
        stepped = fast_state - step_size * gradients_now / grad_rms
        fast_state = stepped * target * lax.rsqrt(lax.optimization_barrier(jnp.mean(stepped * stepped, axis=-1, keepdims=True)) + eps_row)
        applied = fast_state.astype(jnp.bfloat16)
        query_now = query_rows[block_index]
        gate_query = jnp.dot(query_now, applied[0], preferred_element_type=jnp.float32)
        up_query = jnp.dot(query_now, applied[1], preferred_element_type=jnp.float32)
        hidden_query = (gate_query * jax.nn.sigmoid(gate_query) * up_query).astype(jnp.bfloat16)
        results.append(jnp.dot(hidden_query, applied[2], preferred_element_type=jnp.float32).astype(jnp.bfloat16))
    return jnp.stack(results)

def reference(query_tokens, key_tokens, value_tokens, token_rates, fast_init):

    def per_head(array):
        return array.reshape(GROUPS, GROUP, HEADS, HD).transpose(2, 0, 1, 3)
    per_head_out = lax.map(one_head, (per_head(query_tokens), per_head(key_tokens), per_head(value_tokens), token_rates.transpose(2, 0, 1, 3), fast_init.transpose(1, 0, 2, 3)))
    return per_head_out.transpose(1, 2, 0, 3).reshape(GROUPS, GROUP, HEADS * HD)
```

```python
import functools

import jax
import jax.numpy as jnp
from jax import lax
from jax.experimental import pallas as pl
from jax.experimental.pallas import tpu as pltpu
from jax.sharding import PartitionSpec as P

step_size = 0.05
eps_grad = 1e-05
eps_row = 1e-06
MESH = pl.DeviceIdType.MESH
F32 = jnp.float32
BF16 = jnp.bfloat16


def split_of(n):
    core = 2 if n % 2 == 0 else 1
    chips = n // core
    high = next(f for f in (4, 2, 1) if chips % f == 0)
    return core, chips // high, high


def sigmoid(x):
    return 0.5 * jnp.tanh(0.5 * x) + 0.5


def dot(a, b, ca, cb):
    return lax.dot_general(a, b, (((ca,), (cb,)), ((), ())), preferred_element_type=F32)


def kernel(cfg, q_hbm, k_hbm, v_hbm, rates, w_hbm, out, qb, kb, vb, wb, wf, tgt, rt, ab, bb, gf, gb, s1f, s1b, s2f, s2b,
           ra, rb, rc, ag, ob, load_sem, ss, rs, oss, ors, own_sem):
    blocks, heads, tokens, width, per, tile, ncore, nmid, nhi, nhead = cfg
    chunks = heads // per
    rows = per * 3 * width
    wcol = width // ncore
    me = lax.axis_index("seq")
    y = lax.axis_index("head")
    core = lax.rem(me, ncore)
    chip = lax.div(me, ncore)
    mid = lax.rem(chip, nmid)
    hi = lax.div(chip, nmid)

    def seq_id(c, m, h):
        return {"seq": (h * nmid + m) * ncore + c}

    core_peers = [lax.rem(core + d, ncore) for d in range(1, ncore)]
    mid_peers = [lax.rem(mid + d, nmid) for d in range(1, nmid)]
    hi_peers = [lax.rem(hi + d, nhi) for d in range(1, nhi)]
    head_peers = [lax.rem(y + d, nhead) for d in range(1, nhead)]

    loads = {}

    def load(name, src, dst, index):
        loads[name] = pltpu.make_async_copy(src, dst, load_sem.at[index])
        loads[name].start()

    load("w", w_hbm, wb, 0)
    load(("k", 0), k_hbm.at[0], kb.at[0], 1)
    load(("v", 0), v_hbm.at[0], vb.at[0], 2)
    index = 3
    for b in range(blocks):
        if b:
            load(("k", b), k_hbm.at[b], kb.at[b], index)
            load(("v", b), v_hbm.at[b], vb.at[b], index + 1)
            index += 2
        load(("q", b), q_hbm.at[b], qb.at[b], index)
        index += 1

    barrier = pltpu.get_barrier_semaphore()
    ids = [seq_id(c, mid, hi) for c in core_peers] + [seq_id(core, m, hi) for m in mid_peers]
    ids += [seq_id(core, mid, h) for h in hi_peers] + [{"head": p} for p in head_peers]
    for peer in ids:
        pl.semaphore_signal(barrier, inc=1, device_id=peer, device_id_type=MESH)

    lines = [rates[i, b, h:h + 1, :] for i in range(3) for b in range(blocks) for h in range(heads)]
    pad = rt.shape[1] - len(lines)
    if pad:
        lines.append(jnp.zeros((pad, tokens), F32))
    rt[...] = jnp.transpose(jnp.concatenate(lines, axis=0))

    def rate(i, b, h, at):
        column = (i * blocks + b) * heads + h
        return rt[at, column:column + 1]

    loads["w"].wait()
    for h in range(heads):
        for m in range(3):
            w = wb[m, h].astype(F32)
            tgt[h, m] = jnp.sqrt(jnp.mean(w * w, axis=-1, keepdims=True))
            wf[h, m] = w

    pl.semaphore_wait(barrier, len(ids))

    sends = []

    def send(src, dst, sem, peer):
        copy = pltpu.make_async_remote_copy(src_ref=src, dst_ref=dst, send_sem=ss.at[sem], recv_sem=rs.at[sem],
                                            device_id=peer, device_id_type=MESH)
        copy.start()
        sends.append(copy)
        return copy

    base = {}
    at = 0
    for name, count in (("a", ncore - 1), ("b", nmid - 1), ("c", nhi - 1), ("cc", nhi - 1), ("bb", nmid - 1), ("aa", ncore - 1)):
        base[name] = at
        at += count
    per_chunk = at

    def sem_of(name, b, c, d):
        return (b * chunks + c) * per_chunk + base[name] + d

    def grads(b, h):
        cols = slice(h * width, (h + 1) * width)

        def body(i, carry):
            rows_at = pl.ds(pl.multiple_of(i * tile, tile), tile)
            kt = kb[b, rows_at, cols]
            vt = vb[b, rows_at, cols]
            g = dot(kt, wb[0, h], 1, 0)
            u = dot(kt, wb[1, h], 1, 0)
            e = dot(vt, wb[2, h], 1, 1)
            s = sigmoid(g)
            t = g * s
            hidden = (t * u).astype(BF16).astype(F32)
            ab[rows_at, :] = (hidden * rate(2, b, h, rows_at)).astype(BF16)
            dg = e * u * (s + t * (1.0 - s))
            bb[rows_at, :width] = (dg * rate(0, b, h, rows_at)).astype(BF16)
            bb[rows_at, width:] = (e * t * rate(1, b, h, rows_at)).astype(BF16)
            return carry

        lax.fori_loop(0, tokens // tile, body, 0, unroll=True)
        n13 = dot(kb[b, :, cols], bb[...], 0, 0)
        n2 = dot(ab[...], vb[b, :, cols], 0, 0)
        c, row0 = h // per, (h % per) * 3 * width
        for m, value in enumerate((n13[:, :width], n13[:, width:], n2)):
            for j in range(ncore):
                part = value[:, j * wcol:(j + 1) * wcol]
                put = slice(row0 + m * width, row0 + (m + 1) * width)
                gf[c, j, put, :] = part
                gb[b, c, j, put, :] = part.astype(BF16)

    pending = {}

    def start_a(b, c):
        pending["a", b, c] = [send(gb.at[b, c, p], ra.at[b, c, d], sem_of("a", b, c, d), seq_id(p, mid, hi))
                              for d, p in enumerate(core_peers)]

    def finish(name, b, c):
        for copy in pending.pop((name, b, c)):
            copy.wait_recv()

    def start_b(b, c):
        finish("a", b, c)
        total = gf[c, core]
        for d in range(ncore - 1):
            total = total + ra[b, c, d].astype(F32)
        total = total.reshape(s1f.shape[1:])
        s1f[c] = total
        s1b[b, c] = total.astype(BF16)
        pending["b", b, c] = [send(s1b.at[b, c, p], rb.at[b, c, d], sem_of("b", b, c, d), seq_id(core, p, hi))
                              for d, p in enumerate(mid_peers)]

    def start_c(b, c):
        finish("b", b, c)
        total = s1f[c, mid]
        for d in range(nmid - 1):
            total = total + rb[b, c, d].astype(F32)
        s2f[c] = total
        s2b[b, c] = total.astype(BF16)
        pending["c", b, c] = [send(s2b.at[b, c, p], rc.at[b, c, d], sem_of("c", b, c, d), seq_id(core, mid, p))
                              for d, p in enumerate(hi_peers)]

    def start_cc(b, c):
        finish("c", b, c)
        total = s2f[c, hi]
        for d in range(nhi - 1):
            total = total + rc[b, c, d].astype(F32)
        ag[b, c, core, mid, hi] = total.astype(BF16)
        part = ag.at[b, c, core, mid, hi]
        pending["cc", b, c] = [send(part, part, sem_of("cc", b, c, d), seq_id(core, mid, p))
                               for d, p in enumerate(hi_peers)]

    def start_bb(b, c):
        finish("cc", b, c)
        part = ag.at[b, c, core, mid]
        pending["bb", b, c] = [send(part, part, sem_of("bb", b, c, d), seq_id(core, p, hi))
                               for d, p in enumerate(mid_peers)]

    def start_aa(b, c):
        finish("bb", b, c)
        part = ag.at[b, c, core]
        pending["aa", b, c] = [send(part, part, sem_of("aa", b, c, d), seq_id(p, mid, hi))
                               for d, p in enumerate(core_peers)]

    def update(b, c):
        finish("aa", b, c)
        halves = [ag[b, c, j].reshape(rows, wcol) for j in range(ncore)]
        for p in range(per):
            h = c * per + p
            for m in range(3):
                row0 = (p * 3 + m) * width
                n = jnp.concatenate([x[row0:row0 + width].astype(F32) for x in halves], axis=1)
                mean = jnp.sum(jnp.sum(n * n, axis=0, keepdims=True), axis=1, keepdims=True) * (1.0 / (width * width))
                stepped = wf[h, m] + n * (step_size * lax.rsqrt(mean + eps_grad))
                scale = tgt[h, m] * lax.rsqrt(jnp.mean(stepped * stepped, axis=-1, keepdims=True) + eps_row)
                new = stepped * scale
                wf[h, m] = new
                wb[m, h] = new.astype(BF16)

    out_copies = []
    own_copies = []
    part_tokens = tokens // nhead

    def apply(b, h):
        cols = slice(h * width, (h + 1) * width)
        x = qb[b, :, cols]
        g = dot(x, wb[0, h], 1, 0)
        u = dot(x, wb[1, h], 1, 0)
        hq = (g * sigmoid(g) * u).astype(BF16)
        result = dot(hq, wb[2, h], 1, 0).astype(BF16)
        ob[b, h] = result.reshape(nhead, part_tokens, width)
        target = out.at[b, :, pl.ds(pl.multiple_of((y * heads + h) * width, width), width)]
        for d, p in enumerate(head_peers):
            sem = (b * heads + h) * (nhead - 1) + d
            copy = pltpu.make_async_remote_copy(src_ref=ob.at[b, h, p], dst_ref=target, send_sem=oss.at[sem],
                                                recv_sem=ors.at[sem], device_id={"head": p}, device_id_type=MESH)
            copy.start()
            out_copies.append(copy)
        copy = pltpu.make_async_copy(ob.at[b, h, y], target, own_sem.at[b * heads + h])
        copy.start()
        own_copies.append(copy)

    def chunk_heads(c):
        return range(c * per, (c + 1) * per)

    loads["k", 0].wait()
    loads["v", 0].wait()
    for c in range(chunks):
        for h in chunk_heads(c):
            grads(0, h)
        start_a(0, c)
    for b in range(blocks):
        for c in range(chunks):
            start_b(b, c)
        if b:
            for h in range(heads):
                apply(b - 1, h)
        for step in (start_c, start_cc, start_bb, start_aa):
            for c in range(chunks):
                step(b, c)
        loads["q", b].wait()
        if b < blocks - 1:
            loads["k", b + 1].wait()
            loads["v", b + 1].wait()
        for c in range(chunks):
            update(b, c)
            for h in chunk_heads(c):
                if b < blocks - 1:
                    grads(b + 1, h)
                else:
                    apply(b, h)
            if b < blocks - 1:
                start_a(b + 1, c)

    for copy in out_copies:
        copy.wait_recv()
    for copy in own_copies:
        copy.wait()
    for copy in sends + out_copies:
        copy.wait_send()


def solution(mesh):
    nseq, nhead = mesh.shape["seq"], mesh.shape["head"]
    ncore, nmid, nhi = split_of(nseq)

    def body(q, k, v, rates, w):
        blocks, tokens, _ = q.shape
        heads, width = w.shape[1], w.shape[2]
        share = nmid * nhi
        per = next(p for p in range(1, heads + 1) if heads % p == 0 and ((p * 3 * width) % (16 * share) == 0 or p == heads))
        chunks = heads // per
        rows = per * 3 * width
        piece = rows // share
        wcol = width // ncore
        tile = 128 if tokens % 128 == 0 else tokens
        rate_cols = -(-3 * blocks * heads // 8) * 8
        copies = (ncore - 1) + (nmid - 1) + (nhi - 1)
        cfg = (blocks, heads, tokens, width, per, tile, ncore, nmid, nhi, nhead)
        vmem = pltpu.VMEM
        dma = pltpu.SemaphoreType.DMA
        scratch = [
            vmem(q.shape, BF16), vmem(k.shape, BF16), vmem(v.shape, BF16),
            vmem(w.shape, BF16),
            vmem((heads, 3, width, width), F32),
            vmem((heads, 3, width, 1), F32),
            vmem((tokens, rate_cols), F32),
            vmem((tokens, width), BF16),
            vmem((tokens, 2 * width), BF16),
            vmem((chunks, ncore, rows, wcol), F32),
            vmem((blocks, chunks, ncore, rows, wcol), BF16),
            vmem((chunks, nmid, nhi, piece, wcol), F32),
            vmem((blocks, chunks, nmid, nhi, piece, wcol), BF16),
            vmem((chunks, nhi, piece, wcol), F32),
            vmem((blocks, chunks, nhi, piece, wcol), BF16),
            vmem((blocks, chunks, max(ncore - 1, 1), rows, wcol), BF16),
            vmem((blocks, chunks, max(nmid - 1, 1), nhi, piece, wcol), BF16),
            vmem((blocks, chunks, max(nhi - 1, 1), piece, wcol), BF16),
            vmem((blocks, chunks, ncore, nmid, nhi, piece, wcol), BF16),
            vmem((blocks, heads, nhead, tokens // nhead, width), BF16),
            dma((1 + 3 * blocks,)),
            dma((blocks * chunks * 2 * copies,)), dma((blocks * chunks * 2 * copies,)),
            dma((blocks * heads * max(nhead - 1, 1),)), dma((blocks * heads * max(nhead - 1, 1),)),
            dma((blocks * heads,)),
        ]
        anywhere = pl.BlockSpec(memory_space=pl.ANY)
        return pl.pallas_call(
            functools.partial(kernel, cfg),
            out_shape=jax.ShapeDtypeStruct((blocks, tokens // nhead, nhead * heads * width), BF16),
            in_specs=[anywhere, anywhere, anywhere, pl.BlockSpec(memory_space=pltpu.VMEM), anywhere],
            out_specs=anywhere,
            scratch_shapes=scratch,
            compiler_params=pltpu.CompilerParams(collective_id=0, has_side_effects=True,
                                                 vmem_limit_bytes=44 * 1024 * 1024),
        )(q, k, v, rates, w)

    return jax.shard_map(
        body,
        mesh=mesh,
        in_specs=(
            P(None, "seq", "head"),
            P(None, "seq", "head"),
            P(None, "seq", "head"),
            P(None, None, "head", "seq"),
            P(None, "head", None, None),
        ),
        out_specs=P(None, ("seq", "head"), None),
        check_vma=False,
    )
```

```python
import functools
import math

import jax
import jax.numpy as jnp
from jax import lax
from jax.experimental import pallas as pl
from jax.experimental.pallas import tpu as pltpu
from jax.sharding import PartitionSpec as P

step_size = 0.05
eps_grad = 1e-05
eps_row = 1e-06
lanes = 128
MESH = pl.DeviceIdType.MESH
F32 = jnp.float32
BF16 = jnp.bfloat16


def split_of(n, heads):
    core = math.gcd(2, math.gcd(n, heads))
    chips = n // core
    high = next(f for f in (4, 2, 1) if chips % f == 0)
    return core, chips // high, high


def sigmoid(x):
    return 0.5 * jnp.tanh(0.5 * x) + 0.5


def dot(a, b, ca, cb):
    return lax.dot_general(a, b, (((ca,), (cb,)), ((), ())), preferred_element_type=F32)


def kernel(cfg, q_hbm, k_hbm, v_hbm, rates, w_hbm, out, qb, kb, vb, wb, wf, tgt, lb, lr, rt, ab, bb, ob, load_sem, xs, xr, ss, rs,
           oss, ors, own_sem, *chunk_refs):
    blocks, heads, tokens, width, tile, ncore, nmid, nhi, nhead = cfg
    own = heads // ncore
    folds = width // lanes
    me = lax.axis_index("seq")
    y = lax.axis_index("head")
    core = lax.rem(me, ncore)
    chip = lax.div(me, ncore)
    mid = lax.rem(chip, nmid)
    hi = lax.div(chip, nmid)

    def seq_of(c, m, h):
        return (h * nmid + m) * ncore + c

    core_peers = [lax.rem(core + d, ncore) for d in range(1, ncore)]
    mid_peers = [lax.rem(mid + d, nmid) for d in range(1, nmid)]
    hi_peers = [lax.rem(hi + d, nhi) for d in range(1, nhi)]
    out_peers = [(lax.rem(core + dc, ncore), lax.rem(y + dy, nhead)) for dy in range(nhead) for dc in range(ncore) if dc or dy]
    order = list(range(ncore - 1, len(out_peers))) + list(range(ncore - 1))

    def mid_id(p):
        return {"seq": seq_of(core, p, hi)}

    def hi_id(p):
        return {"seq": seq_of(core, mid, p)}

    def out_id(p):
        return {"seq": seq_of(p[0], mid, hi), "head": p[1]}

    barrier = pltpu.get_barrier_semaphore()
    ids = [out_id(p) for p in out_peers] + [mid_id(p) for p in mid_peers] + [hi_id(p) for p in hi_peers]
    for peer in ids:
        pl.semaphore_signal(barrier, inc=1, device_id=peer, device_id_type=MESH)

    loads = {}

    def head_cols(c):
        return pl.ds(pl.multiple_of(c * (own * width), lanes), own * width)

    loads["w"] = pltpu.make_async_copy(w_hbm.at[:, pl.ds(core * own, own)], wb, load_sem.at[0])
    loads["w"].start()
    arrays = {"k": (k_hbm, kb), "v": (v_hbm, vb), "q": (q_hbm, qb)}
    names = [("k", 0), ("v", 0)]
    for b in range(blocks):
        names += [("k", b + 1), ("v", b + 1), ("q", b)] if b < blocks - 1 else [("q", b)]
    for i, (name, b) in enumerate(names):
        src, dst = arrays[name]
        loads[name, b] = pltpu.make_async_copy(src.at[b, :, head_cols(core)], dst.at[b, core], load_sem.at[1 + i])
        loads[name, b].start()

    count = 3 * blocks * own
    for dc in range(ncore):
        c = lax.rem(core + dc, ncore)
        lines = [rates[i, b, pl.ds(c * own + h, 1), :] for i in range(3) for b in range(blocks) for h in range(own)]
        if lb.shape[1] > count:
            lines.append(jnp.zeros((lb.shape[1] - count, tokens), F32))
        lb[dc] = jnp.concatenate(lines, axis=0)

    pl.semaphore_wait(barrier, len(ids))

    sends = []
    gifts = {}

    def gift(key, src, dst, p, sem):
        copy = pltpu.make_async_remote_copy(src_ref=src, dst_ref=dst, send_sem=xs.at[sem], recv_sem=xr.at[sem],
                                            device_id={"seq": seq_of(p, mid, hi)}, device_id_type=MESH)
        copy.start()
        sends.append(copy)
        gifts.setdefault(key, []).append(copy)

    for d, p in enumerate(core_peers):
        first = d * (1 + len(names))
        gift("rates", lb.at[d + 1], lr.at[d], p, first)
        for i, (name, b) in enumerate(names):
            src, dst = arrays[name]
            gift((name, b), src.at[b, :, head_cols(p)], dst.at[b, core], p, first + 1 + i)

    rt[core] = jnp.transpose(lb[0])
    loads["w"].wait()
    for h in range(own):
        for m in range(3):
            w = wb[m, h].astype(F32)
            tgt[h, m] = jnp.sqrt(jnp.mean(w * w, axis=-1, keepdims=True))
            wf[h, m] = w

    def arrived(key):
        for copy in gifts.get(key, ()):
            copy.wait_recv()

    per_chunk = 2 * (nmid - 1 + nhi - 1)
    refs = {}
    for b in range(blocks):
        for h in range(own):
            for m in range(3):
                i = (h * 3 + m) * 7
                refs[b, h, m] = [r.at[b] for r in chunk_refs[i:i + 7]]

    def sides(m):
        one, two = (nmid, mid, mid_peers, mid_id), (nhi, hi, hi_peers, hi_id)
        return (one, two) if m < 2 else (two, one)

    pending = {}

    def exchange(key, number, pairs, peers, id_of):
        b, h, m = key
        copies = []
        for d, p in enumerate(peers):
            src, dst = pairs(d, p)
            sem = ((b * own + h) * 3 + m) * per_chunk + number + d
            copy = pltpu.make_async_remote_copy(src_ref=src, dst_ref=dst, send_sem=ss.at[sem], recv_sem=rs.at[sem],
                                                device_id=id_of(p), device_id_type=MESH)
            copy.start()
            copies.append(copy)
        sends.extend(copies)
        pending[key] = copies

    def finish(key):
        for copy in pending.pop(key):
            copy.wait_recv()

    def start_first(key, value):
        gf, gb, r1, sf, sb, r2, ag = refs[key]
        (n1, _, peers, id_of), _ = sides(key[2])
        folded = jnp.concatenate([value[:, j * lanes:(j + 1) * lanes] for j in range(folds)], axis=0).reshape(gf.shape)
        gf[...] = folded
        gb[...] = folded.astype(BF16)
        exchange(key, 0, lambda d, p: (gb.at[p], r1.at[d]), peers, id_of)

    def start_second(key):
        finish(key)
        gf, gb, r1, sf, sb, r2, ag = refs[key]
        (n1, my1, peers1, _), (n2, my2, peers, id_of) = sides(key[2])
        total = gf[my1]
        for d in range(n1 - 1):
            total = total + r1[d].astype(F32)
        sf[...] = total
        sb[...] = total.astype(BF16)
        exchange(key, n1 - 1, lambda d, p: (sb.at[p], r2.at[d]), peers, id_of)

    def start_third(key):
        finish(key)
        gf, gb, r1, sf, sb, r2, ag = refs[key]
        (n1, my1, _, _), (n2, my2, peers, id_of) = sides(key[2])
        total = sf[my2]
        for d in range(n2 - 1):
            total = total + r2[d].astype(F32)
        ag[my1, my2] = total.astype(BF16)
        part = ag.at[my1, my2]
        exchange(key, n1 + n2 - 2, lambda d, p: (part, part), peers, id_of)

    def start_fourth(key):
        finish(key)
        ag = refs[key][6]
        (n1, my1, peers, id_of), (n2, _, _, _) = sides(key[2])
        part = ag.at[my1]
        exchange(key, n1 + 2 * n2 - 3, lambda d, p: (part, part), peers, id_of)

    def update(key):
        finish(key)
        b, h, m = key
        x = refs[key][6][...].reshape(folds * width, lanes)
        n = jnp.concatenate([x[j * width:(j + 1) * width].astype(F32) for j in range(folds)], axis=1)
        mean = jnp.sum(jnp.sum(n * n, axis=0, keepdims=True), axis=1, keepdims=True) * (1.0 / (width * width))
        stepped = wf[h, m] + n * (step_size * lax.rsqrt(mean + eps_grad))
        new = stepped * (tgt[h, m] * lax.rsqrt(jnp.mean(stepped * stepped, axis=-1, keepdims=True) + eps_row))
        wf[h, m] = new
        wb[m, h] = new.astype(BF16)

    def grads(b, h):
        cols = slice(h * width, (h + 1) * width)

        def part(c):
            def body(i, carry):
                at = pl.ds(pl.multiple_of(i * tile, tile), tile)
                kt = kb[b, c, at, cols]
                vt = vb[b, c, at, cols]
                g = dot(kt, wb[0, h], 1, 0)
                u = dot(kt, wb[1, h], 1, 0)
                e = dot(vt, wb[2, h], 1, 1)

                def rate(i):
                    column = (i * blocks + b) * own + h
                    return rt[c, at, column:column + 1]

                s = sigmoid(g)
                t = g * s
                hidden = (t * u).astype(BF16).astype(F32)
                ab[c, at, :] = (hidden * rate(2)).astype(BF16)
                dg = e * u * (s + t * (1.0 - s))
                bb[c, at, :width] = (dg * rate(0)).astype(BF16)
                bb[c, at, width:] = (e * t * rate(1)).astype(BF16)
                return carry

            lax.fori_loop(0, tokens // tile, body, 0, unroll=True)

        if h == 0:
            loads["k", b].wait()
            loads["v", b].wait()
        part(core)
        for d, p in enumerate(core_peers):
            if h == 0 and d == 0:
                arrived(("k", b))
                arrived(("v", b))
                if b == 0:
                    arrived("rates")
                    for e, other in enumerate(core_peers):
                        rt[lax.rem(core + ncore - 1 - e, ncore)] = jnp.transpose(lr[e])
            part(p)
        flat = ncore * tokens
        start_first((b, h, 2), dot(ab[...].reshape(flat, width), vb[b, :, :, cols].reshape(flat, width), 0, 0))
        n13 = dot(kb[b, :, :, cols].reshape(flat, width), bb[...].reshape(flat, 2 * width), 0, 0)
        start_first((b, h, 0), n13[:, :width])
        start_first((b, h, 1), n13[:, width:])

    part_tokens = tokens // nhead
    out_copies = []
    own_copies = []

    def apply(b):
        loads["q", b].wait()
        arrived(("q", b))
        target = out.at[b, :, pl.ds(pl.multiple_of((y * heads + core * own) * width, lanes), own * width)]

        def rows_of(c, part):
            at = pl.ds(pl.multiple_of(part * part_tokens, part_tokens), part_tokens)
            for h in range(own):
                cols = slice(h * width, (h + 1) * width)
                x = qb[b, c, at, cols]
                g = dot(x, wb[0, h], 1, 0)
                u = dot(x, wb[1, h], 1, 0)
                hq = (g * sigmoid(g) * u).astype(BF16)
                ob[b, c, part, :, cols] = dot(hq, wb[2, h], 1, 0).astype(BF16)

        for d in order:
            p = out_peers[d]
            rows_of(*p)
            sem = b * len(out_peers) + d
            copy = pltpu.make_async_remote_copy(src_ref=ob.at[b, p[0], p[1]], dst_ref=target, send_sem=oss.at[sem],
                                                recv_sem=ors.at[sem], device_id=out_id(p), device_id_type=MESH)
            copy.start()
            out_copies.append(copy)
        rows_of(core, y)
        copy = pltpu.make_async_copy(ob.at[b, core, y], target, own_sem.at[b])
        copy.start()
        own_copies.append(copy)

    for h in range(own):
        grads(0, h)
    for b in range(blocks):
        turn = (2, 0, 1)
        keys = [(b, h, m) for h in range(own) for m in turn]
        for key in keys:
            start_second(key)
        if b:
            apply(b - 1)
        for step in (start_third, start_fourth):
            for key in keys:
                step(key)
        if b < blocks - 1:
            for h in range(own):
                for m in turn:
                    update((b, h, m))
                grads(b + 1, h)
        else:
            for key in keys:
                update(key)
            apply(b)

    for copy in out_copies:
        copy.wait_recv()
    for copy in own_copies:
        copy.wait()
    for copy in sends + out_copies:
        copy.wait_send()


def solution(mesh):
    nseq, nhead = mesh.shape["seq"], mesh.shape["head"]

    def body(q, k, v, rates, w):
        blocks, tokens, _ = q.shape
        heads, width = w.shape[1], w.shape[2]
        ncore, nmid, nhi = split_of(nseq, heads)
        own = heads // ncore
        tile = 128 if tokens % 128 == 0 else tokens
        cfg = (blocks, heads, tokens, width, tile, ncore, nmid, nhi, nhead)
        vmem = pltpu.VMEM
        dma = pltpu.SemaphoreType.DMA
        loads = 3 * blocks
        others = max(ncore - 1, 1)
        lines = -(-3 * blocks * own // 8) * 8
        copies = blocks * own * 3 * 2 * (nmid - 1 + nhi - 1)
        out_copies = blocks * (ncore * nhead - 1)
        scratch = [
            *[vmem((blocks, ncore, tokens, own * width), BF16)] * 3,
            vmem((3, own, width, width), BF16),
            vmem((own, 3, width, width), F32),
            vmem((own, 3, width, 1), F32),
            vmem((ncore, lines, tokens), F32),
            vmem((others, lines, tokens), F32),
            vmem((ncore, tokens, lines), F32),
            vmem((ncore, tokens, width), BF16),
            vmem((ncore, tokens, 2 * width), BF16),
            vmem((blocks, ncore, nhead, tokens // nhead, own * width), BF16),
            dma((1 + loads,)),
            *[dma((others * (1 + loads),))] * 2,
            *[dma((copies,))] * 2,
            *[dma((out_copies,))] * 2,
            dma((blocks,)),
        ]
        piece = width * width // lanes // (nmid * nhi)
        for _ in range(own):
            for m in range(3):
                n1, n2 = (nmid, nhi) if m < 2 else (nhi, nmid)
                scratch += [
                    vmem((blocks, n1, n2, piece, lanes), F32),
                    vmem((blocks, n1, n2, piece, lanes), BF16),
                    vmem((blocks, max(n1 - 1, 1), n2, piece, lanes), BF16),
                    vmem((blocks, n2, piece, lanes), F32),
                    vmem((blocks, n2, piece, lanes), BF16),
                    vmem((blocks, max(n2 - 1, 1), piece, lanes), BF16),
                    vmem((blocks, n1, n2, piece, lanes), BF16),
                ]
        anywhere = pl.BlockSpec(memory_space=pl.ANY)
        return pl.pallas_call(
            functools.partial(kernel, cfg),
            out_shape=jax.ShapeDtypeStruct((blocks, tokens // nhead, nhead * heads * width), BF16),
            in_specs=[anywhere, anywhere, anywhere, pl.BlockSpec(memory_space=pltpu.VMEM), anywhere],
            out_specs=anywhere,
            scratch_shapes=scratch,
            compiler_params=pltpu.CompilerParams(collective_id=0, has_side_effects=True,
                                                 vmem_limit_bytes=62 * 1024 * 1024),
        )(q, k, v, rates, w)

    return jax.shard_map(
        body,
        mesh=mesh,
        in_specs=(
            P(None, "seq", "head"),
            P(None, "seq", "head"),
            P(None, "seq", "head"),
            P(None, None, "head", "seq"),
            P(None, "head", None, None),
        ),
        out_specs=P(None, ("seq", "head"), None),
        check_vma=False,
    )
```

```python
import functools
import math

import jax
import jax.numpy as jnp
from jax import lax
from jax.experimental import pallas as pl
from jax.experimental.pallas import tpu as pltpu
from jax.sharding import PartitionSpec as P

step_size = 0.05
eps_grad = 1e-05
eps_row = 1e-06
lanes = 128
MESH = pl.DeviceIdType.MESH
F32 = jnp.float32
BF16 = jnp.bfloat16


def split_of(n, heads):
    core = math.gcd(2, math.gcd(n, heads))
    chips = n // core
    high = next(f for f in (4, 2, 1) if chips % f == 0)
    return core, chips // high, high


def sigmoid(x):
    return 0.5 * jnp.tanh(0.5 * x) + 0.5


def dot(a, b, ca, cb):
    return lax.dot_general(a, b, (((ca,), (cb,)), ((), ())), preferred_element_type=F32)


def kernel(cfg, q_hbm, k_hbm, v_hbm, rates, w_hbm, out, qb, kb, vb, wb, wf, tgt, lb, lr, rt, ab, bb, ob, load_sem, xs, xr, ss, rs,
           oss, ors, own_sem, *chunk_refs):
    blocks, heads, tokens, width, tile, ncore, nmid, nhi, nhead, subs = cfg
    own = heads // ncore
    folds = width // lanes // subs
    parts = 3 * subs
    me = lax.axis_index("seq")
    y = lax.axis_index("head")
    core = lax.rem(me, ncore)
    chip = lax.div(me, ncore)
    mid = lax.rem(chip, nmid)
    hi = lax.div(chip, nmid)

    def seq_of(c, m, h):
        return (h * nmid + m) * ncore + c

    core_peers = [lax.rem(core + d, ncore) for d in range(1, ncore)]
    mid_peers = [lax.rem(mid + d, nmid) for d in range(1, nmid)]
    hi_peers = [lax.rem(hi + d, nhi) for d in range(1, nhi)]
    out_peers = [(lax.rem(core + dc, ncore), lax.rem(y + dy, nhead)) for dy in range(nhead) for dc in range(ncore) if dc or dy]
    order = list(range(ncore - 1, len(out_peers))) + list(range(ncore - 1))

    def mid_id(p):
        return {"seq": seq_of(core, p, hi)}

    def hi_id(p):
        return {"seq": seq_of(core, mid, p)}

    def out_id(p):
        return {"seq": seq_of(p[0], mid, hi), "head": p[1]}

    barrier = pltpu.get_barrier_semaphore()
    ids = [out_id(p) for p in out_peers] + [mid_id(p) for p in mid_peers] + [hi_id(p) for p in hi_peers]
    for peer in ids:
        pl.semaphore_signal(barrier, inc=1, device_id=peer, device_id_type=MESH)

    loads = {}

    def head_cols(c):
        return pl.ds(pl.multiple_of(c * (own * width), lanes), own * width)

    loads["w"] = pltpu.make_async_copy(w_hbm.at[:, pl.ds(core * own, own)], wb, load_sem.at[0])
    loads["w"].start()
    arrays = {"k": (k_hbm, kb), "v": (v_hbm, vb), "q": (q_hbm, qb)}
    names = [("k", 0), ("v", 0)]
    for b in range(blocks):
        names += [("k", b + 1), ("v", b + 1), ("q", b)] if b < blocks - 1 else [("q", b)]
    for i, (name, b) in enumerate(names):
        src, dst = arrays[name]
        loads[name, b] = pltpu.make_async_copy(src.at[b, :, head_cols(core)], dst.at[b, core], load_sem.at[1 + i])
        loads[name, b].start()

    count = 3 * blocks * own
    for dc in range(ncore):
        c = lax.rem(core + dc, ncore)
        lines = [rates[i, b, pl.ds(c * own + h, 1), :] for i in range(3) for b in range(blocks) for h in range(own)]
        if lb.shape[1] > count:
            lines.append(jnp.zeros((lb.shape[1] - count, tokens), F32))
        lb[dc] = jnp.concatenate(lines, axis=0)

    pl.semaphore_wait(barrier, len(ids))

    sends = []
    gifts = {}

    def gift(key, src, dst, p, sem):
        copy = pltpu.make_async_remote_copy(src_ref=src, dst_ref=dst, send_sem=xs.at[sem], recv_sem=xr.at[sem],
                                            device_id={"seq": seq_of(p, mid, hi)}, device_id_type=MESH)
        copy.start()
        sends.append(copy)
        gifts.setdefault(key, []).append(copy)

    for d, p in enumerate(core_peers):
        first = d * (1 + len(names))
        gift("rates", lb.at[d + 1], lr.at[d], p, first)
        for i, (name, b) in enumerate(names):
            src, dst = arrays[name]
            gift((name, b), src.at[b, :, head_cols(p)], dst.at[b, core], p, first + 1 + i)

    rt[core] = jnp.transpose(lb[0])
    loads["w"].wait()
    for h in range(own):
        for m in range(3):
            w = wb[m, h].astype(F32)
            tgt[h, m] = jnp.sqrt(jnp.mean(w * w, axis=-1, keepdims=True))
            wf[h, m] = w

    def arrived(key):
        for copy in gifts.get(key, ()):
            copy.wait_recv()

    per_chunk = 2 * (nmid - 1 + nhi - 1)
    refs = {}
    for b in range(blocks):
        for h in range(own):
            for m in range(parts):
                i = (h * parts + m) * 7
                refs[b, h, m] = [r.at[b] for r in chunk_refs[i:i + 7]]

    def sides(m):
        one, two = (nmid, mid, mid_peers, mid_id), (nhi, hi, hi_peers, hi_id)
        return (one, two) if m < 3 * subs - subs // 2 else (two, one)

    pending = {}

    def exchange(key, number, pairs, peers, id_of):
        b, h, m = key
        copies = []
        for d, p in enumerate(peers):
            src, dst = pairs(d, p)
            sem = ((b * own + h) * parts + m) * per_chunk + number + d
            copy = pltpu.make_async_remote_copy(src_ref=src, dst_ref=dst, send_sem=ss.at[sem], recv_sem=rs.at[sem],
                                                device_id=id_of(p), device_id_type=MESH)
            copy.start()
            copies.append(copy)
        sends.extend(copies)
        pending[key] = copies

    def finish(key):
        for copy in pending.pop(key):
            copy.wait_recv()

    def start_first(key, value):
        gf, gb, r1, sf, sb, r2, ag = refs[key]
        (n1, _, peers, id_of), _ = sides(key[2])
        first = key[2] % subs * folds
        folded = [value[:, j * lanes:(j + 1) * lanes] for j in range(first, first + folds)]
        folded = jnp.concatenate(folded, axis=0).reshape(gf.shape)
        gf[...] = folded
        gb[...] = folded.astype(BF16)
        exchange(key, 0, lambda d, p: (gb.at[p], r1.at[d]), peers, id_of)

    def start_second(key):
        finish(key)
        gf, gb, r1, sf, sb, r2, ag = refs[key]
        (n1, my1, peers1, _), (n2, my2, peers, id_of) = sides(key[2])
        total = gf[my1]
        for d in range(n1 - 1):
            total = total + r1[d].astype(F32)
        sf[...] = total
        sb[...] = total.astype(BF16)
        exchange(key, n1 - 1, lambda d, p: (sb.at[p], r2.at[d]), peers, id_of)

    def start_third(key):
        finish(key)
        gf, gb, r1, sf, sb, r2, ag = refs[key]
        (n1, my1, _, _), (n2, my2, peers, id_of) = sides(key[2])
        total = sf[my2]
        for d in range(n2 - 1):
            total = total + r2[d].astype(F32)
        ag[my1, my2] = total.astype(BF16)
        part = ag.at[my1, my2]
        exchange(key, n1 + n2 - 2, lambda d, p: (part, part), peers, id_of)

    def start_fourth(key):
        finish(key)
        ag = refs[key][6]
        (n1, my1, peers, id_of), (n2, _, _, _) = sides(key[2])
        part = ag.at[my1]
        exchange(key, n1 + 2 * n2 - 3, lambda d, p: (part, part), peers, id_of)

    def update(key):
        b, h, m = key
        n = []
        for j in range(subs):
            part = (b, h, m * subs + j)
            finish(part)
            x = refs[part][6][...].reshape(folds * width, lanes)
            n += [x[i * width:(i + 1) * width].astype(F32) for i in range(folds)]
        n = jnp.concatenate(n, axis=1)
        mean = jnp.sum(jnp.sum(n * n, axis=0, keepdims=True), axis=1, keepdims=True) * (1.0 / (width * width))
        stepped = wf[h, m] + n * (step_size * lax.rsqrt(mean + eps_grad))
        new = stepped * (tgt[h, m] * lax.rsqrt(jnp.mean(stepped * stepped, axis=-1, keepdims=True) + eps_row))
        wf[h, m] = new
        wb[m, h] = new.astype(BF16)

    def grads(b, h):
        cols = slice(h * width, (h + 1) * width)

        def part(c):
            def body(i, carry):
                at = pl.ds(pl.multiple_of(i * tile, tile), tile)
                kt = kb[b, c, at, cols]
                vt = vb[b, c, at, cols]
                g = dot(kt, wb[0, h], 1, 0)
                u = dot(kt, wb[1, h], 1, 0)
                e = dot(vt, wb[2, h], 1, 1)

                def rate(i):
                    column = (i * blocks + b) * own + h
                    return rt[c, at, column:column + 1]

                s = sigmoid(g)
                t = g * s
                hidden = (t * u).astype(BF16).astype(F32)
                ab[c, at, :] = (hidden * rate(2)).astype(BF16)
                dg = e * u * (s + t * (1.0 - s))
                bb[c, at, :width] = (dg * rate(0)).astype(BF16)
                bb[c, at, width:] = (e * t * rate(1)).astype(BF16)
                return carry

            lax.fori_loop(0, tokens // tile, body, 0, unroll=True)

        if h == 0:
            loads["k", b].wait()
            loads["v", b].wait()
        part(core)
        for d, p in enumerate(core_peers):
            if h == 0 and d == 0:
                arrived(("k", b))
                arrived(("v", b))
                if b == 0:
                    arrived("rates")
                    for e, other in enumerate(core_peers):
                        rt[lax.rem(core + ncore - 1 - e, ncore)] = jnp.transpose(lr[e])
            part(p)
        flat = ncore * tokens
        n2 = dot(ab[...].reshape(flat, width), vb[b, :, :, cols].reshape(flat, width), 0, 0)
        for j in range(subs):
            start_first((b, h, 2 * subs + j), n2)
        n13 = dot(kb[b, :, :, cols].reshape(flat, width), bb[...].reshape(flat, 2 * width), 0, 0)
        for m in range(2):
            for j in range(subs):
                start_first((b, h, m * subs + j), n13[:, m * width:(m + 1) * width])

    part_tokens = tokens // nhead
    out_copies = []
    own_copies = []

    def apply(b):
        loads["q", b].wait()
        arrived(("q", b))
        target = out.at[b, :, pl.ds(pl.multiple_of((y * heads + core * own) * width, lanes), own * width)]

        def rows_of(c, part):
            at = pl.ds(pl.multiple_of(part * part_tokens, part_tokens), part_tokens)
            for h in range(own):
                cols = slice(h * width, (h + 1) * width)
                x = qb[b, c, at, cols]
                g = dot(x, wb[0, h], 1, 0)
                u = dot(x, wb[1, h], 1, 0)
                hq = (g * sigmoid(g) * u).astype(BF16)
                ob[b, c, part, :, cols] = dot(hq, wb[2, h], 1, 0).astype(BF16)

        for d in order:
            p = out_peers[d]
            rows_of(*p)
            sem = b * len(out_peers) + d
            copy = pltpu.make_async_remote_copy(src_ref=ob.at[b, p[0], p[1]], dst_ref=target, send_sem=oss.at[sem],
                                                recv_sem=ors.at[sem], device_id=out_id(p), device_id_type=MESH)
            copy.start()
            out_copies.append(copy)
        rows_of(core, y)
        copy = pltpu.make_async_copy(ob.at[b, core, y], target, own_sem.at[b])
        copy.start()
        own_copies.append(copy)

    for h in range(own):
        grads(0, h)
    for b in range(blocks):
        turn = (2, 0, 1)
        keys = [(b, h, m * subs + j) for h in range(own) for m in turn for j in range(subs)]
        for key in keys:
            start_second(key)
        if b:
            apply(b - 1)
        for step in (start_third, start_fourth):
            for key in keys:
                step(key)
        if b < blocks - 1:
            for h in range(own):
                for m in turn:
                    update((b, h, m))
                grads(b + 1, h)
        else:
            for h in range(own):
                for m in turn:
                    update((b, h, m))
            apply(b)

    for copy in out_copies:
        copy.wait_recv()
    for copy in own_copies:
        copy.wait()
    for copy in sends + out_copies:
        copy.wait_send()


def solution(mesh):
    nseq, nhead = mesh.shape["seq"], mesh.shape["head"]

    def body(q, k, v, rates, w):
        blocks, tokens, _ = q.shape
        heads, width = w.shape[1], w.shape[2]
        ncore, nmid, nhi = split_of(nseq, heads)
        own = heads // ncore
        tile = 128 if tokens % 128 == 0 else tokens
        folds = width // lanes
        share = nmid * nhi
        subs = next(n for n in range(folds, 0, -1) if folds % n == 0 and (folds // n * width % (16 * share) == 0 or n == 1))
        cfg = (blocks, heads, tokens, width, tile, ncore, nmid, nhi, nhead, subs)
        vmem = pltpu.VMEM
        dma = pltpu.SemaphoreType.DMA
        loads = 3 * blocks
        others = max(ncore - 1, 1)
        lines = -(-3 * blocks * own // 8) * 8
        copies = blocks * own * 3 * subs * 2 * (nmid - 1 + nhi - 1)
        out_copies = blocks * (ncore * nhead - 1)
        scratch = [
            *[vmem((blocks, ncore, tokens, own * width), BF16)] * 3,
            vmem((3, own, width, width), BF16),
            vmem((own, 3, width, width), F32),
            vmem((own, 3, width, 1), F32),
            vmem((ncore, lines, tokens), F32),
            vmem((others, lines, tokens), F32),
            vmem((ncore, tokens, lines), F32),
            vmem((ncore, tokens, width), BF16),
            vmem((ncore, tokens, 2 * width), BF16),
            vmem((blocks, ncore, nhead, tokens // nhead, own * width), BF16),
            dma((1 + loads,)),
            *[dma((others * (1 + loads),))] * 2,
            *[dma((copies,))] * 2,
            *[dma((out_copies,))] * 2,
            dma((blocks,)),
        ]
        piece = width * folds // subs // share
        for _ in range(own):
            for m in range(3 * subs):
                n1, n2 = (nmid, nhi) if m < 3 * subs - subs // 2 else (nhi, nmid)
                scratch += [
                    vmem((blocks, n1, n2, piece, lanes), F32),
                    vmem((blocks, n1, n2, piece, lanes), BF16),
                    vmem((blocks, max(n1 - 1, 1), n2, piece, lanes), BF16),
                    vmem((blocks, n2, piece, lanes), F32),
                    vmem((blocks, n2, piece, lanes), BF16),
                    vmem((blocks, max(n2 - 1, 1), piece, lanes), BF16),
                    vmem((blocks, n1, n2, piece, lanes), BF16),
                ]
        anywhere = pl.BlockSpec(memory_space=pl.ANY)
        return pl.pallas_call(
            functools.partial(kernel, cfg),
            out_shape=jax.ShapeDtypeStruct((blocks, tokens // nhead, nhead * heads * width), BF16),
            in_specs=[anywhere, anywhere, anywhere, pl.BlockSpec(memory_space=pltpu.VMEM), anywhere],
            out_specs=anywhere,
            scratch_shapes=scratch,
            compiler_params=pltpu.CompilerParams(collective_id=0, has_side_effects=True,
                                                 vmem_limit_bytes=62 * 1024 * 1024),
        )(q, k, v, rates, w)

    return jax.shard_map(
        body,
        mesh=mesh,
        in_specs=(
            P(None, "seq", "head"),
            P(None, "seq", "head"),
            P(None, "seq", "head"),
            P(None, None, "head", "seq"),
            P(None, "head", None, None),
        ),
        out_specs=P(None, ("seq", "head"), None),
        check_vma=False,
    )
```

```python
import functools
import math

import jax
import jax.numpy as jnp
from jax import lax
from jax.experimental import pallas as pl
from jax.experimental.pallas import tpu as pltpu
from jax.sharding import PartitionSpec as P

step_size = 0.05
eps_grad = 1e-05
eps_row = 1e-06
lanes = 128
MESH = pl.DeviceIdType.MESH
F32 = jnp.float32
BF16 = jnp.bfloat16


def split_of(n, heads):
    core = math.gcd(2, math.gcd(n, heads))
    chips = n // core
    high = next(f for f in (4, 2, 1) if chips % f == 0)
    return core, chips // high, high


def sigmoid(x):
    return 0.5 * jnp.tanh(0.5 * x) + 0.5


def dot(a, b, ca, cb):
    return lax.dot_general(a, b, (((ca,), (cb,)), ((), ())), preferred_element_type=F32)


def kernel(cfg, q_hbm, k_hbm, v_hbm, rates, w_hbm, out, qb, kb, vb, wb, wf, tgt, lb, lr, rt, ab, bb, ob, load_sem, xs, xr, ss, rs,
           oss, ors, own_sem, *chunk_refs):
    blocks, heads, tokens, width, tile, ncore, nmid, nhi, nhead, subs = cfg
    own = heads // ncore
    folds = width // lanes // subs
    parts = 3 * subs
    me = lax.axis_index("seq")
    y = lax.axis_index("head")
    core = lax.rem(me, ncore)
    chip = lax.div(me, ncore)
    mid = lax.rem(chip, nmid)
    hi = lax.div(chip, nmid)

    def seq_of(c, m, h):
        return (h * nmid + m) * ncore + c

    core_peers = [lax.rem(core + d, ncore) for d in range(1, ncore)]
    mid_peers = [lax.rem(mid + d, nmid) for d in range(1, nmid)]
    hi_peers = [lax.rem(hi + d, nhi) for d in range(1, nhi)]
    out_peers = [(lax.rem(core + dc, ncore), lax.rem(y + dy, nhead)) for dy in range(nhead) for dc in range(ncore) if dc or dy]
    order = list(range(ncore - 1, len(out_peers))) + list(range(ncore - 1))

    def mid_id(p):
        return {"seq": seq_of(core, p, hi)}

    def hi_id(p):
        return {"seq": seq_of(core, mid, p)}

    def out_id(p):
        return {"seq": seq_of(p[0], mid, hi), "head": p[1]}

    barrier = pltpu.get_barrier_semaphore()
    ids = [out_id(p) for p in out_peers] + [mid_id(p) for p in mid_peers] + [hi_id(p) for p in hi_peers]
    for peer in ids:
        pl.semaphore_signal(barrier, inc=1, device_id=peer, device_id_type=MESH)

    loads = {}

    def head_cols(c):
        return pl.ds(pl.multiple_of(c * (own * width), lanes), own * width)

    loads["w"] = pltpu.make_async_copy(w_hbm.at[:, pl.ds(core * own, own)], wb, load_sem.at[0])
    loads["w"].start()
    arrays = {"k": (k_hbm, kb), "v": (v_hbm, vb), "q": (q_hbm, qb)}
    names = [("k", 0), ("v", 0)]
    for b in range(blocks):
        names += [("k", b + 1), ("v", b + 1), ("q", b)] if b < blocks - 1 else [("q", b)]
    for i, (name, b) in enumerate(names):
        src, dst = arrays[name]
        loads[name, b] = pltpu.make_async_copy(src.at[b, :, head_cols(core)], dst.at[b, core], load_sem.at[1 + i])
        loads[name, b].start()

    count = 3 * blocks * own
    for dc in range(ncore):
        c = lax.rem(core + dc, ncore)
        lines = [rates[i, b, pl.ds(c * own + h, 1), :] for i in range(3) for b in range(blocks) for h in range(own)]
        if lb.shape[1] > count:
            lines.append(jnp.zeros((lb.shape[1] - count, tokens), F32))
        lb[dc] = jnp.concatenate(lines, axis=0)

    pl.semaphore_wait(barrier, len(ids))

    sends = []
    gifts = {}

    def gift(key, src, dst, p, sem):
        copy = pltpu.make_async_remote_copy(src_ref=src, dst_ref=dst, send_sem=xs.at[sem], recv_sem=xr.at[sem],
                                            device_id={"seq": seq_of(p, mid, hi)}, device_id_type=MESH)
        copy.start()
        sends.append(copy)
        gifts.setdefault(key, []).append(copy)

    for d, p in enumerate(core_peers):
        first = d * (1 + len(names))
        gift("rates", lb.at[d + 1], lr.at[d], p, first)
        for i, (name, b) in enumerate(names):
            src, dst = arrays[name]
            gift((name, b), src.at[b, :, head_cols(p)], dst.at[b, core], p, first + 1 + i)

    rt[core] = jnp.transpose(lb[0])
    loads["w"].wait()
    for h in range(own):
        for m in range(3):
            w = wb[m, h].astype(F32)
            tgt[h, m] = jnp.sqrt(jnp.mean(w * w, axis=-1, keepdims=True))
            wf[h, m] = w

    def arrived(key):
        for copy in gifts.get(key, ()):
            copy.wait_recv()

    per_chunk = 2 * (nmid - 1 + nhi - 1)
    refs = {}
    for b in range(blocks):
        for h in range(own):
            for m in range(parts):
                i = (h * parts + m) * 7
                refs[b, h, m] = [r.at[b] for r in chunk_refs[i:i + 7]]

    def sides(m):
        one, two = (nmid, mid, mid_peers, mid_id), (nhi, hi, hi_peers, hi_id)
        return (one, two) if m < 3 * subs - subs // 2 else (two, one)

    pending = {}

    def exchange(key, number, pairs, peers, id_of):
        b, h, m = key
        copies = []
        for d, p in enumerate(peers):
            src, dst = pairs(d, p)
            sem = ((b * own + h) * parts + m) * per_chunk + number + d
            copy = pltpu.make_async_remote_copy(src_ref=src, dst_ref=dst, send_sem=ss.at[sem], recv_sem=rs.at[sem],
                                                device_id=id_of(p), device_id_type=MESH)
            copy.start()
            copies.append(copy)
        sends.extend(copies)
        pending[key] = copies

    def finish(key):
        for copy in pending.pop(key):
            copy.wait_recv()

    def start_first(key, value):
        gf, gb, r1, sf, sb, r2, ag = refs[key]
        (n1, _, peers, id_of), _ = sides(key[2])
        first = key[2] % subs * folds
        folded = [value[:, j * lanes:(j + 1) * lanes] for j in range(first, first + folds)]
        folded = jnp.concatenate(folded, axis=0).reshape(gf.shape)
        gf[...] = folded
        gb[...] = folded.astype(BF16)
        exchange(key, 0, lambda d, p: (gb.at[p], r1.at[d]), peers, id_of)

    def start_second(key):
        finish(key)
        gf, gb, r1, sf, sb, r2, ag = refs[key]
        (n1, my1, peers1, _), (n2, my2, peers, id_of) = sides(key[2])
        total = gf[my1]
        for d in range(n1 - 1):
            total = total + r1[d].astype(F32)
        sf[...] = total
        sb[...] = total.astype(BF16)
        exchange(key, n1 - 1, lambda d, p: (sb.at[p], r2.at[d]), peers, id_of)

    def start_third(key):
        finish(key)
        gf, gb, r1, sf, sb, r2, ag = refs[key]
        (n1, my1, _, _), (n2, my2, peers, id_of) = sides(key[2])
        total = sf[my2]
        for d in range(n2 - 1):
            total = total + r2[d].astype(F32)
        ag[my1, my2] = total.astype(BF16)
        part = ag.at[my1, my2]
        exchange(key, n1 + n2 - 2, lambda d, p: (part, part), peers, id_of)

    def start_fourth(key):
        finish(key)
        ag = refs[key][6]
        (n1, my1, peers, id_of), (n2, _, _, _) = sides(key[2])
        part = ag.at[my1]
        exchange(key, n1 + 2 * n2 - 3, lambda d, p: (part, part), peers, id_of)

    def update(key):
        b, h, m = key
        n = []
        for j in range(subs):
            part = (b, h, m * subs + j)
            finish(part)
            x = refs[part][6][...].reshape(folds * width, lanes)
            n += [x[i * width:(i + 1) * width].astype(F32) for i in range(folds)]
        n = jnp.concatenate(n, axis=1)
        mean = jnp.sum(jnp.sum(n * n, axis=0, keepdims=True), axis=1, keepdims=True) * (1.0 / (width * width))
        stepped = wf[h, m] + n * (step_size * lax.rsqrt(mean + eps_grad))
        new = stepped * (tgt[h, m] * lax.rsqrt(jnp.mean(stepped * stepped, axis=-1, keepdims=True) + eps_row))
        wf[h, m] = new
        wb[m, h] = new.astype(BF16)

    def grads(b, h):
        cols = slice(h * width, (h + 1) * width)

        def part(c):
            def body(i, carry):
                at = pl.ds(pl.multiple_of(i * tile, tile), tile)
                kt = kb[b, c, at, cols]
                vt = vb[b, c, at, cols]
                g = dot(kt, wb[0, h], 1, 0)
                u = dot(kt, wb[1, h], 1, 0)
                e = dot(vt, wb[2, h], 1, 1)

                def rate(i):
                    column = (i * blocks + b) * own + h
                    return rt[c, at, column:column + 1]

                s = sigmoid(g)
                t = g * s
                hidden = (t * u).astype(BF16).astype(F32)
                ab[c, at, :] = (hidden * rate(2)).astype(BF16)
                dg = e * u * (s + t * (1.0 - s))
                bb[c, at, :width] = (dg * rate(0)).astype(BF16)
                bb[c, at, width:] = (e * t * rate(1)).astype(BF16)
                return carry

            lax.fori_loop(0, tokens // tile, body, 0, unroll=True)

        if h == 0:
            loads["k", b].wait()
            loads["v", b].wait()
        part(core)
        for d, p in enumerate(core_peers):
            if h == 0 and d == 0:
                arrived(("k", b))
                arrived(("v", b))
                if b == 0:
                    arrived("rates")
                    for e, other in enumerate(core_peers):
                        rt[lax.rem(core + ncore - 1 - e, ncore)] = jnp.transpose(lr[e])
            part(p)
        flat = ncore * tokens
        n2 = dot(ab[...].reshape(flat, width), vb[b, :, :, cols].reshape(flat, width), 0, 0)
        for j in range(subs):
            start_first((b, h, 2 * subs + j), n2)
        n13 = dot(kb[b, :, :, cols].reshape(flat, width), bb[...].reshape(flat, 2 * width), 0, 0)
        for m in range(2):
            for j in range(subs):
                start_first((b, h, m * subs + j), n13[:, m * width:(m + 1) * width])

    part_tokens = tokens // nhead
    out_copies = []
    own_copies = []

    def apply(b):
        loads["q", b].wait()
        arrived(("q", b))
        target = out.at[b, :, pl.ds(pl.multiple_of((y * heads + core * own) * width, lanes), own * width)]

        def rows_of(c, part):
            at = pl.ds(pl.multiple_of(part * part_tokens, part_tokens), part_tokens)
            for h in range(own):
                cols = slice(h * width, (h + 1) * width)
                x = qb[b, c, at, cols]
                g = dot(x, wb[0, h], 1, 0)
                u = dot(x, wb[1, h], 1, 0)
                hq = (g * sigmoid(g) * u).astype(BF16)
                ob[b, c, part, :, cols] = dot(hq, wb[2, h], 1, 0).astype(BF16)

        for d in order:
            p = out_peers[d]
            rows_of(*p)
            sem = b * len(out_peers) + d
            copy = pltpu.make_async_remote_copy(src_ref=ob.at[b, p[0], p[1]], dst_ref=target, send_sem=oss.at[sem],
                                                recv_sem=ors.at[sem], device_id=out_id(p), device_id_type=MESH)
            copy.start()
            out_copies.append(copy)
        rows_of(core, y)
        copy = pltpu.make_async_copy(ob.at[b, core, y], target, own_sem.at[b])
        copy.start()
        own_copies.append(copy)

    for h in range(own):
        grads(0, h)
    for b in range(blocks):
        turn = (2, 0, 1)
        keys = [(b, h, m * subs + j) for h in range(own) for m in turn for j in range(subs)]
        for key in keys:
            start_second(key)
        for key in keys:
            start_third(key)
        if b:
            apply(b - 1)
        for key in keys:
            start_fourth(key)
        if b < blocks - 1:
            for h in range(own):
                for m in turn:
                    update((b, h, m))
                grads(b + 1, h)
        else:
            for h in range(own):
                for m in turn:
                    update((b, h, m))
            apply(b)

    for copy in out_copies:
        copy.wait_recv()
    for copy in own_copies:
        copy.wait()
    for copy in sends + out_copies:
        copy.wait_send()


def solution(mesh):
    nseq, nhead = mesh.shape["seq"], mesh.shape["head"]

    def body(q, k, v, rates, w):
        blocks, tokens, _ = q.shape
        heads, width = w.shape[1], w.shape[2]
        ncore, nmid, nhi = split_of(nseq, heads)
        own = heads // ncore
        tile = 128 if tokens % 128 == 0 else tokens
        folds = width // lanes
        share = nmid * nhi
        subs = next(n for n in range(folds, 0, -1) if folds % n == 0 and (folds // n * width % (16 * share) == 0 or n == 1))
        cfg = (blocks, heads, tokens, width, tile, ncore, nmid, nhi, nhead, subs)
        vmem = pltpu.VMEM
        dma = pltpu.SemaphoreType.DMA
        loads = 3 * blocks
        others = max(ncore - 1, 1)
        lines = -(-3 * blocks * own // 8) * 8
        copies = blocks * own * 3 * subs * 2 * (nmid - 1 + nhi - 1)
        out_copies = blocks * (ncore * nhead - 1)
        scratch = [
            *[vmem((blocks, ncore, tokens, own * width), BF16)] * 3,
            vmem((3, own, width, width), BF16),
            vmem((own, 3, width, width), F32),
            vmem((own, 3, width, 1), F32),
            vmem((ncore, lines, tokens), F32),
            vmem((others, lines, tokens), F32),
            vmem((ncore, tokens, lines), F32),
            vmem((ncore, tokens, width), BF16),
            vmem((ncore, tokens, 2 * width), BF16),
            vmem((blocks, ncore, nhead, tokens // nhead, own * width), BF16),
            dma((1 + loads,)),
            *[dma((others * (1 + loads),))] * 2,
            *[dma((copies,))] * 2,
            *[dma((out_copies,))] * 2,
            dma((blocks,)),
        ]
        piece = width * folds // subs // share
        for _ in range(own):
            for m in range(3 * subs):
                n1, n2 = (nmid, nhi) if m < 3 * subs - subs // 2 else (nhi, nmid)
                scratch += [
                    vmem((blocks, n1, n2, piece, lanes), F32),
                    vmem((blocks, n1, n2, piece, lanes), BF16),
                    vmem((blocks, max(n1 - 1, 1), n2, piece, lanes), BF16),
                    vmem((blocks, n2, piece, lanes), F32),
                    vmem((blocks, n2, piece, lanes), BF16),
                    vmem((blocks, max(n2 - 1, 1), piece, lanes), BF16),
                    vmem((blocks, n1, n2, piece, lanes), BF16),
                ]
        anywhere = pl.BlockSpec(memory_space=pl.ANY)
        return pl.pallas_call(
            functools.partial(kernel, cfg),
            out_shape=jax.ShapeDtypeStruct((blocks, tokens // nhead, nhead * heads * width), BF16),
            in_specs=[anywhere, anywhere, anywhere, pl.BlockSpec(memory_space=pltpu.VMEM), anywhere],
            out_specs=anywhere,
            scratch_shapes=scratch,
            compiler_params=pltpu.CompilerParams(collective_id=0, has_side_effects=True,
                                                 vmem_limit_bytes=62 * 1024 * 1024),
        )(q, k, v, rates, w)

    return jax.shard_map(
        body,
        mesh=mesh,
        in_specs=(
            P(None, "seq", "head"),
            P(None, "seq", "head"),
            P(None, "seq", "head"),
            P(None, None, "head", "seq"),
            P(None, "head", None, None),
        ),
        out_specs=P(None, ("seq", "head"), None),
        check_vma=False,
    )
```
